32 devices in a mesh: prow: 4 (over z), pcol: 8 (over y, x, core).
Axes of the slice: x: 2, y: 2, z: 4, core: 2. Of those that a mesh axis runs over, the one named last changes fastest.
Arguments:
- ancestor_inv: float32 [16384, 16384], P('prow', 'pcol'), may hold values from -0.15625 to 0.15625
- l_scaled: float32 [2, 1536, 512], P(None, 'prow'), may hold values from -0.9 to 0.9
- diag_inv: float32 [2, 512, 512], replicated, may hold values from -6 to 6
- tile_lists: int32 [2, 6], replicated, may hold values from 0 to 63, as said below
Outputs:
- offdiag: float32 [2, 1536, 512], P(None, ('prow', 'pcol'))
- diag_block: float32 [2, 512, 512], replicated
The draws below stay inside these ranges and needn't reach their ends.
Inputs may be any that keep to these rules, and one draw needn't show every extreme that they name: `tile_lists`: each row holds 6 different tile numbers; tile 0 and tile 64 - 1 are in every row.
All inputs are finite; a program needn't handle non-finite values.
Results may differ from the reference program's by a relative error of at most 0.0001.
Values sent between devices are 32-bit elements; how exact they have to be, the bound alone decides.
A program may use at most 192 MiB of HBM per device.

```python
import jax
import jax.numpy as jnp
from jax import lax

TILE = 256
W = 512
NT = 64
NS = 6
NSUP = 2
ORDER = 16384
ROWS = 1536


def draw_tile_lists(key, part):

    def single(sub):
        first, second = jax.random.split(sub)
        middle = 1 + jax.random.permutation(first, NT - 2)[:NS - 2]
        ends = jnp.array([0, NT - 1], dtype=jnp.int32)
        whole = jnp.concatenate([ends, middle.astype(jnp.int32)])
        return jax.random.permutation(second, whole)
    keys = jax.random.split(jax.random.fold_in(key, 7), NSUP)
    return jax.vmap(single)(keys).astype(jnp.int32)


def block_levels(stream_key, shape, pieces, least, top_value):
    loudness = 1.0
    for axis_at, parts in pieces:
        draws = jax.random.uniform(jax.random.fold_in(jax.random.fold_in(stream_key, 6), axis_at), (parts,), jnp.float32, least / len(pieces), top_value / len(pieces))
        loudness = loudness * jnp.repeat(jnp.exp(draws), shape[axis_at] // parts).reshape((-1,) + (1,) * (len(shape) - 1 - axis_at))
    return loudness


def scatter_about(rng, dims, width, most, cuts=(), kind=jnp.bfloat16):
    drawn = jax.random.normal(rng, dims, jnp.float32) * width
    if len(cuts) > 0:
        drawn = block_levels(rng, dims, cuts, -0.22, 0.18) * drawn
    return jnp.clip(drawn, min=-most, max=most).astype(kind)


def setup_inputs(seed: int = 0) -> dict:
    key_list = jax.random.split(jax.random.key(seed), 5)
    return {
        "ancestor_inv": scatter_about(key_list[0], (ORDER, ORDER), (NS * TILE) ** -0.5, 0.15625, ((0, 4), (1, 8)), jnp.float32),
        "l_scaled": scatter_about(key_list[1], (NSUP, ROWS, W), 0.15, 0.9, ((1, 4),), jnp.float32),
        "diag_inv": scatter_about(key_list[2], (NSUP, W, W), 1.0, 6.0, (), jnp.float32),
        "tile_lists": draw_tile_lists(jax.random.fold_in(key_list[4], 71), 0),
    }


def reference(ancestor_inv, l_scaled, diag_inv, tile_lists):
    offs = []
    diags = []
    within = jnp.arange(TILE, dtype=jnp.int32)
    for index in range(NSUP):
        rows_k = (tile_lists[index][:, None] * TILE + within[None, :]).reshape(-1).astype(jnp.int32)
        block = ancestor_inv[rows_k][:, rows_k]
        result = -jnp.dot(block, l_scaled[index], precision=lax.Precision.HIGHEST, preferred_element_type=jnp.float32)
        offs.append(result)
        term = jnp.dot(l_scaled[index].T, result, precision=lax.Precision.HIGHEST, preferred_element_type=jnp.float32)
        diags.append(diag_inv[index] - term)
    return jnp.stack(offs), jnp.stack(diags)
```

```python
import functools

import jax
import jax.numpy as jnp
from jax import lax
from jax.experimental import pallas as pl
from jax.experimental.pallas import tpu as pltpu
from jax.sharding import PartitionSpec as P

TILE = 256
W = 512
NS = 6
NSUP = 2
MESH = pl.DeviceIdType.MESH


def place(stage):
    row = lax.axis_index("prow")
    col = lax.axis_index("pcol")
    core = lax.rem(col, 2)
    chip = col // 2
    if stage == "row":
        return row, lambda m: (m, col)
    if stage == "chip":
        return chip, lambda m: (row, m * 2 + core)
    return core, lambda m: (row, chip * 2 + m)


def exchange_kernel(stage, size, scatter, x_ref, out_ref, send_sem, recv_sem, own_sem):
    me, device = place(stage)
    barrier = pltpu.get_barrier_semaphore()
    for step in range(1, size):
        pl.semaphore_signal(
            barrier, inc=1, device_id=device(lax.rem(me + step, size)), device_id_type=MESH
        )
    pl.semaphore_wait(barrier, size - 1)
    copies = []
    for step in range(1, size):
        to = lax.rem(me + step, size)
        copy = pltpu.make_async_remote_copy(
            src_ref=x_ref.at[to] if scatter else x_ref,
            dst_ref=out_ref.at[me],
            send_sem=send_sem.at[step - 1],
            recv_sem=recv_sem.at[step - 1],
            device_id=device(to),
            device_id_type=MESH,
        )
        copy.start()
        copies.append(copy)
    own = pltpu.make_async_copy(x_ref.at[me] if scatter else x_ref, out_ref.at[me], own_sem)
    own.start()
    own.wait()
    for copy in copies:
        copy.wait()


def exchange(x, stage, size, scatter, collective_id):
    shape = x.shape if scatter else (size,) + x.shape
    return pl.pallas_call(
        functools.partial(exchange_kernel, stage, size, scatter),
        out_shape=jax.ShapeDtypeStruct(shape, x.dtype),
        in_specs=[pl.BlockSpec(memory_space=pl.ANY)],
        out_specs=pl.BlockSpec(memory_space=pl.ANY),
        scratch_shapes=[
            pltpu.SemaphoreType.DMA((size - 1,)),
            pltpu.SemaphoreType.DMA((size - 1,)),
            pltpu.SemaphoreType.DMA,
        ],
        compiler_params=pltpu.CompilerParams(
            collective_id=collective_id, has_side_effects=True
        ),
    )(x)


def product_kernel(rows_ref, cols_ref, a_ref, l_ref, p_ref, d_ref):
    sup, i, j = pl.program_id(0), pl.program_id(1), pl.program_id(2)
    highest = lax.Precision.HIGHEST
    row_hit = rows_ref[sup, i] >= 0

    @pl.when((i == 0) & (j == 0))
    def _():
        d_ref[...] = jnp.zeros_like(d_ref)

    @pl.when(j == 0)
    def _():
        p_ref[...] = jnp.zeros_like(p_ref)

    @pl.when(row_hit & (cols_ref[sup, j] >= 0))
    def _():
        block = l_ref[0, pl.ds(pl.multiple_of(j * TILE, TILE), TILE), :]
        p_ref[0] -= jnp.dot(
            a_ref[...], block, precision=highest, preferred_element_type=jnp.float32
        )

    @pl.when(row_hit & (j == NS - 1))
    def _():
        block = l_ref[0, pl.ds(pl.multiple_of(i * TILE, TILE), TILE), :]
        d_ref[0] += lax.dot_general(
            block,
            p_ref[0],
            (((0,), (0,)), ((), ())),
            precision=highest,
            preferred_element_type=jnp.float32,
        )


def products(rows, cols, ancestor, lfull):
    def a_map(sup, i, j, rows_ref, cols_ref):
        row, col = rows_ref[sup, i], cols_ref[sup, j]
        hit = (row >= 0) & (col >= 0)
        return jnp.where(hit, row, 0), jnp.where(hit, col, 0)

    total = lfull.shape[1]
    return pl.pallas_call(
        product_kernel,
        out_shape=(
            jax.ShapeDtypeStruct((NSUP, total, W), jnp.float32),
            jax.ShapeDtypeStruct((NSUP, W, W), jnp.float32),
        ),
        grid_spec=pltpu.PrefetchScalarGridSpec(
            num_scalar_prefetch=2,
            grid=(NSUP, NS, NS),
            in_specs=[
                pl.BlockSpec((TILE, TILE), a_map),
                pl.BlockSpec((1, total, W), lambda sup, i, j, *_: (sup, 0, 0)),
            ],
            out_specs=[
                pl.BlockSpec((1, TILE, W), lambda sup, i, j, *_: (sup, i, 0)),
                pl.BlockSpec((1, W, W), lambda sup, i, j, *_: (sup, 0, 0)),
            ],
        ),
        compiler_params=pltpu.CompilerParams(vmem_limit_bytes=40 * 1024 * 1024),
    )(rows, cols, ancestor, lfull)


def per_device(nrow, ncol, ancestor_inv, l_scaled, diag_inv, tile_lists):
    nchip = ncol // 2
    tile_rows = ancestor_inv.shape[0] // TILE
    tile_cols = ancestor_inv.shape[1] // TILE
    row_pos = lax.axis_index("prow")
    col_pos = lax.axis_index("pcol")
    count = l_scaled.shape[1] // ncol
    part = W // (nrow * ncol)
    total = l_scaled.shape[1] * nrow

    share = lax.dynamic_slice_in_dim(l_scaled, col_pos * count, count, 1)
    held = exchange(share, "row", nrow, False, 1)
    held = exchange(held, "chip", nchip, False, 2)
    held = exchange(held, "core", 2, False, 3)
    lfull = held.transpose(3, 2, 1, 0, 4, 5).reshape(NSUP, total, W)

    rows = tile_lists - row_pos * tile_rows
    rows = jnp.where((rows >= 0) & (rows < tile_rows), rows, -1)
    cols = tile_lists - col_pos * tile_cols
    cols = jnp.where((cols >= 0) & (cols < tile_cols), cols, -1)
    partial, terms = products(rows, cols, ancestor_inv, lfull)

    partial = partial.reshape(NSUP, nrow, nchip, 2, count, W)
    terms = terms.reshape(NSUP, nrow, nchip, 2, part, W)
    sums = jnp.concatenate([partial, terms], axis=4).transpose(3, 2, 1, 0, 4, 5)
    sums = exchange(sums, "core", 2, True, 4).sum(0)
    sums = exchange(sums, "chip", nchip, True, 5).sum(0)
    sums = exchange(sums, "row", nrow, True, 6).sum(0)
    mine = sums[:, :count]

    diag = exchange(sums[:, count:], "row", nrow, False, 7)
    diag = exchange(diag, "chip", nchip, False, 8)
    diag = exchange(diag, "core", 2, False, 9)
    diag = diag.transpose(3, 2, 1, 0, 4, 5).reshape(NSUP, W, W)
    return mine, diag_inv - diag


def solution(mesh):
    placed = (P("prow", "pcol"), P(None, "prow", None), P(), P())
    return jax.shard_map(
        functools.partial(per_device, mesh.shape["prow"], mesh.shape["pcol"]),
        mesh=mesh,
        in_specs=placed,
        out_specs=(P(None, ("prow", "pcol"), None), P()),
        check_vma=False,
    )
```

```python
import functools

import jax
import jax.numpy as jnp
from jax import lax
from jax.experimental import pallas as pl
from jax.experimental.pallas import tpu as pltpu
from jax.sharding import PartitionSpec as P

TILE = 256
W = 512
NS = 6
NSUP = 2
MESH = pl.DeviceIdType.MESH


def place(stage):
    row = lax.axis_index("prow")
    col = lax.axis_index("pcol")
    core = lax.rem(col, 2)
    chip = col // 2
    if stage == "row":
        return row, lambda m: (m, col)
    if stage == "chip":
        return chip, lambda m: (row, m * 2 + core)
    return core, lambda m: (row, chip * 2 + m)


def exchange_kernel(stage, size, scatter, x_ref, out_ref, send_sem, recv_sem):
    me, device = place(stage)
    barrier = pltpu.get_barrier_semaphore()
    for step in range(1, size):
        pl.semaphore_signal(
            barrier, inc=1, device_id=device(lax.rem(me + step, size)), device_id_type=MESH
        )
    pl.semaphore_wait(barrier, size - 1)
    copies = []
    for step in range(1, size):
        to = lax.rem(me + step, size)
        copy = pltpu.make_async_remote_copy(
            src_ref=x_ref.at[to] if scatter else x_ref,
            dst_ref=out_ref.at[me],
            send_sem=send_sem.at[step - 1],
            recv_sem=recv_sem.at[step - 1],
            device_id=device(to),
            device_id_type=MESH,
        )
        copy.start()
        copies.append(copy)
    for copy in copies:
        copy.wait()


def exchange(x, stage, size, scatter, collective_id):
    shape = x.shape if scatter else (size,) + x.shape
    moved = pl.pallas_call(
        functools.partial(exchange_kernel, stage, size, scatter),
        out_shape=jax.ShapeDtypeStruct(shape, x.dtype),
        in_specs=[pl.BlockSpec(memory_space=pl.ANY)],
        out_specs=pl.BlockSpec(memory_space=pl.ANY),
        scratch_shapes=[
            pltpu.SemaphoreType.DMA((size - 1,)),
            pltpu.SemaphoreType.DMA((size - 1,)),
        ],
        compiler_params=pltpu.CompilerParams(
            collective_id=collective_id, has_side_effects=True
        ),
    )(x)
    me, _ = place(stage)
    if not scatter:
        return lax.dynamic_update_index_in_dim(moved, x, me, 0)
    own = lax.dynamic_index_in_dim(x, me, 0, keepdims=False)
    for step in range(1, size):
        own += lax.dynamic_index_in_dim(moved, lax.rem(me + step, size), 0, keepdims=False)
    return own


def product_kernel(rows_ref, cols_ref, a_ref, l_ref, p_ref, d_ref):
    sup, i, j = pl.program_id(0), pl.program_id(1), pl.program_id(2)
    highest = lax.Precision.HIGHEST
    row_hit = rows_ref[sup, i] >= 0

    @pl.when((i == 0) & (j == 0))
    def _():
        d_ref[...] = jnp.zeros_like(d_ref)

    @pl.when(j == 0)
    def _():
        p_ref[...] = jnp.zeros_like(p_ref)

    @pl.when(row_hit & (cols_ref[sup, j] >= 0))
    def _():
        block = l_ref[0, pl.ds(pl.multiple_of(j * TILE, TILE), TILE), :]
        p_ref[0] -= jnp.dot(
            a_ref[...], block, precision=highest, preferred_element_type=jnp.float32
        )

    @pl.when(row_hit & (j == NS - 1))
    def _():
        block = l_ref[0, pl.ds(pl.multiple_of(i * TILE, TILE), TILE), :]
        d_ref[0] += lax.dot_general(
            block,
            p_ref[0],
            (((0,), (0,)), ((), ())),
            precision=highest,
            preferred_element_type=jnp.float32,
        )


def products(rows, cols, ancestor, lfull):
    def a_map(sup, i, j, rows_ref, cols_ref):
        row, col = rows_ref[sup, i], cols_ref[sup, j]
        hit = (row >= 0) & (col >= 0)
        return jnp.where(hit, row, 0), jnp.where(hit, col, 0)

    total = lfull.shape[1]
    return pl.pallas_call(
        product_kernel,
        out_shape=(
            jax.ShapeDtypeStruct((NSUP, total, W), jnp.float32),
            jax.ShapeDtypeStruct((NSUP, W, W), jnp.float32),
        ),
        grid_spec=pltpu.PrefetchScalarGridSpec(
            num_scalar_prefetch=2,
            grid=(NSUP, NS, NS),
            in_specs=[
                pl.BlockSpec((TILE, TILE), a_map),
                pl.BlockSpec((1, total, W), lambda sup, i, j, *_: (sup, 0, 0)),
            ],
            out_specs=[
                pl.BlockSpec((1, TILE, W), lambda sup, i, j, *_: (sup, i, 0)),
                pl.BlockSpec((1, W, W), lambda sup, i, j, *_: (sup, 0, 0)),
            ],
        ),
        compiler_params=pltpu.CompilerParams(vmem_limit_bytes=40 * 1024 * 1024),
    )(rows, cols, ancestor, lfull)


def per_device(nrow, ncol, ancestor_inv, l_scaled, diag_inv, tile_lists):
    nchip = ncol // 2
    tile_rows = ancestor_inv.shape[0] // TILE
    tile_cols = ancestor_inv.shape[1] // TILE
    row_pos = lax.axis_index("prow")
    col_pos = lax.axis_index("pcol")
    count = l_scaled.shape[1] // ncol
    part = W // (nrow * ncol)
    total = l_scaled.shape[1] * nrow

    share = lax.dynamic_slice_in_dim(l_scaled, col_pos * count, count, 1)
    held = exchange(share, "row", nrow, False, 1)
    held = exchange(held, "chip", nchip, False, 2)
    held = exchange(held, "core", 2, False, 3)
    lfull = held.transpose(3, 2, 1, 0, 4, 5).reshape(NSUP, total, W)

    rows = tile_lists - row_pos * tile_rows
    rows = jnp.where((rows >= 0) & (rows < tile_rows), rows, -1)
    cols = tile_lists - col_pos * tile_cols
    cols = jnp.where((cols >= 0) & (cols < tile_cols), cols, -1)
    partial, terms = products(rows, cols, ancestor_inv, lfull)

    partial = partial.reshape(NSUP, nrow, nchip, 2, count, W)
    terms = terms.reshape(NSUP, nrow, nchip, 2, part, W)
    sums = jnp.concatenate([partial, terms], axis=4).transpose(3, 2, 1, 0, 4, 5)
    sums = exchange(sums, "core", 2, True, 4)
    sums = exchange(sums, "chip", nchip, True, 5)
    sums = exchange(sums, "row", nrow, True, 6)
    mine = sums[:, :count]

    diag = exchange(sums[:, count:], "row", nrow, False, 7)
    diag = exchange(diag, "chip", nchip, False, 8)
    diag = exchange(diag, "core", 2, False, 9)
    diag = diag.transpose(3, 2, 1, 0, 4, 5).reshape(NSUP, W, W)
    return mine, diag_inv - diag


def solution(mesh):
    placed = (P("prow", "pcol"), P(None, "prow", None), P(), P())
    return jax.shard_map(
        functools.partial(per_device, mesh.shape["prow"], mesh.shape["pcol"]),
        mesh=mesh,
        in_specs=placed,
        out_specs=(P(None, ("prow", "pcol"), None), P()),
        check_vma=False,
    )
```

```python
import functools

import jax
import jax.numpy as jnp
from jax import lax
from jax.experimental import pallas as pl
from jax.experimental.pallas import tpu as pltpu
from jax.sharding import PartitionSpec as P

TILE = 256
W = 512
NS = 6
NSUP = 2
MESH = pl.DeviceIdType.MESH


def place(stage):
    row = lax.axis_index("prow")
    col = lax.axis_index("pcol")
    core = lax.rem(col, 2)
    chip = col // 2
    if stage == "row":
        return row, lambda m: (m, col)
    if stage == "chip":
        return chip, lambda m: (row, m * 2 + core)
    return core, lambda m: (row, chip * 2 + m)


def enter(peers):
    barrier = pltpu.get_barrier_semaphore()
    for peer in peers:
        pl.semaphore_signal(barrier, inc=1, device_id=peer, device_id_type=MESH)
    pl.semaphore_wait(barrier, len(peers))


def others(stage, size):
    me, device = place(stage)
    return [device(lax.rem(me + step, size)) for step in range(1, size)]


def scatter_kernel(stage, size, axis, x_ref, y_ref, x_out, y_out, send_sem, recv_sem):
    me, _ = place(stage)
    peers = others(stage, size)
    enter(peers)
    copies = []
    lead = (slice(None),) * axis
    for step, peer in enumerate(peers):
        to = lax.rem(me + step + 1, size)
        for which, (src, dst) in enumerate(((x_ref, x_out), (y_ref, y_out))):
            copy = pltpu.make_async_remote_copy(
                src_ref=src.at[lead + (to,)],
                dst_ref=dst.at[step],
                send_sem=send_sem.at[step, which],
                recv_sem=recv_sem.at[step, which],
                device_id=peer,
                device_id_type=MESH,
            )
            copy.start()
            copies.append(copy)
    for copy in copies:
        copy.wait()


def scatter(pair, stage, size, axis, collective_id):
    shapes = [(size - 1,) + x.shape[:axis] + x.shape[axis + 1:] for x in pair]
    moved = pl.pallas_call(
        functools.partial(scatter_kernel, stage, size, axis),
        out_shape=[jax.ShapeDtypeStruct(shape, jnp.float32) for shape in shapes],
        in_specs=[pl.BlockSpec(memory_space=pl.ANY)] * 2,
        out_specs=[pl.BlockSpec(memory_space=pl.ANY)] * 2,
        scratch_shapes=[
            pltpu.SemaphoreType.DMA((size - 1, 2)),
            pltpu.SemaphoreType.DMA((size - 1, 2)),
        ],
        compiler_params=pltpu.CompilerParams(
            collective_id=collective_id, has_side_effects=True
        ),
    )(*pair)
    me, _ = place(stage)
    sums = []
    for x, parts in zip(pair, moved):
        own = lax.dynamic_index_in_dim(x, me, axis, keepdims=False)
        for step in range(size - 1):
            own += parts[step]
        sums.append(own)
    return sums


def gather_kernel(nrow, nchip, x_ref, out_ref, *sems):
    row_send, row_recv, chip_send, chip_recv, core_send, core_recv = sems
    row, _ = place("row")
    chip, _ = place("chip")
    core, _ = place("core")
    rows, chips, cores = others("row", nrow), others("chip", nchip), others("core", 2)
    enter(rows + chips + cores)
    started = []

    def send(src, slot, send_sem, recv_sem, peer):
        copy = pltpu.make_async_remote_copy(
            src_ref=src,
            dst_ref=slot,
            send_sem=send_sem,
            recv_sem=recv_sem,
            device_id=peer,
            device_id_type=MESH,
        )
        copy.start()
        started.append(copy)
        return copy

    mine = out_ref.at[:, row, chip, core]
    from_rows = [
        send(x_ref, mine, row_send.at[step], row_recv.at[step], peer)
        for step, peer in enumerate(rows)
    ]
    from_chips = []
    last = []
    for near in range(nrow):
        src = x_ref
        slot = mine
        if near > 0:
            from_rows[near - 1].wait_recv()
            slot = out_ref.at[:, lax.rem(row - near + nrow, nrow), chip, core]
            src = slot
        for step, peer in enumerate(chips):
            from_chips.append(
                (
                    near,
                    step + 1,
                    send(src, slot, chip_send.at[step, near], chip_recv.at[step, near], peer),
                )
            )
        last.append(send(src, slot, core_send.at[0, near], core_recv.at[0, near], cores[0]))
    for near, step, copy in from_chips:
        copy.wait_recv()
        slot = out_ref.at[
            :, lax.rem(row - near + nrow, nrow), lax.rem(chip - step + nchip, nchip), core
        ]
        last.append(
            send(slot, slot, core_send.at[step, near], core_recv.at[step, near], cores[0])
        )
    for copy in last:
        copy.wait_recv()
    for copy in started:
        copy.wait_send()


def gather(x, nrow, nchip, collective_id):
    shape = (x.shape[0], nrow, nchip, 2) + x.shape[1:]
    row, chip, core = ((nrow - 1,), (nchip - 1, nrow), (nchip, nrow))
    full = pl.pallas_call(
        functools.partial(gather_kernel, nrow, nchip),
        out_shape=jax.ShapeDtypeStruct(shape, x.dtype),
        in_specs=[pl.BlockSpec(memory_space=pl.ANY)],
        out_specs=pl.BlockSpec(memory_space=pl.ANY),
        scratch_shapes=[
            pltpu.SemaphoreType.DMA(n) for n in (row, row, chip, chip, core, core)
        ],
        compiler_params=pltpu.CompilerParams(
            collective_id=collective_id, has_side_effects=True
        ),
    )(x)
    where = (0, place("row")[0], place("chip")[0], place("core")[0], 0, 0)
    return lax.dynamic_update_slice(full, x[:, None, None, None], where)


def product_kernel(rows_ref, cols_ref, a_ref, l_ref, p_ref, d_ref):
    sup, i, j = pl.program_id(0), pl.program_id(1), pl.program_id(2)
    highest = lax.Precision.HIGHEST
    row_hit = rows_ref[sup, i] >= 0

    @pl.when((i == 0) & (j == 0))
    def _():
        d_ref[...] = jnp.zeros_like(d_ref)

    @pl.when(j == 0)
    def _():
        p_ref[...] = jnp.zeros_like(p_ref)

    @pl.when(row_hit & (cols_ref[sup, j] >= 0))
    def _():
        block = l_ref[0, pl.ds(pl.multiple_of(j * TILE, TILE), TILE), :]
        p_ref[0] -= jnp.dot(
            a_ref[...], block, precision=highest, preferred_element_type=jnp.float32
        )

    @pl.when(row_hit & (j == NS - 1))
    def _():
        block = l_ref[0, pl.ds(pl.multiple_of(i * TILE, TILE), TILE), :]
        d_ref[0] += lax.dot_general(
            block,
            p_ref[0],
            (((0,), (0,)), ((), ())),
            precision=highest,
            preferred_element_type=jnp.float32,
        )


def products(rows, cols, ancestor, lfull):
    def a_map(sup, i, j, rows_ref, cols_ref):
        row, col = rows_ref[sup, i], cols_ref[sup, j]
        hit = (row >= 0) & (col >= 0)
        return jnp.where(hit, row, 0), jnp.where(hit, col, 0)

    total = lfull.shape[1]
    return pl.pallas_call(
        product_kernel,
        out_shape=(
            jax.ShapeDtypeStruct((NSUP, total, W), jnp.float32),
            jax.ShapeDtypeStruct((NSUP, W, W), jnp.float32),
        ),
        grid_spec=pltpu.PrefetchScalarGridSpec(
            num_scalar_prefetch=2,
            grid=(NSUP, NS, NS),
            in_specs=[
                pl.BlockSpec((TILE, TILE), a_map),
                pl.BlockSpec((1, total, W), lambda sup, i, j, *_: (sup, 0, 0)),
            ],
            out_specs=[
                pl.BlockSpec((1, TILE, W), lambda sup, i, j, *_: (sup, i, 0)),
                pl.BlockSpec((1, W, W), lambda sup, i, j, *_: (sup, 0, 0)),
            ],
        ),
        compiler_params=pltpu.CompilerParams(vmem_limit_bytes=40 * 1024 * 1024),
    )(rows, cols, ancestor, lfull)


def per_device(nrow, ncol, ancestor_inv, l_scaled, diag_inv, tile_lists):
    nchip = ncol // 2
    tile_rows = ancestor_inv.shape[0] // TILE
    tile_cols = ancestor_inv.shape[1] // TILE
    row_pos = lax.axis_index("prow")
    col_pos = lax.axis_index("pcol")
    count = l_scaled.shape[1] // ncol
    part = W // (nrow * ncol)
    total = l_scaled.shape[1] * nrow

    share = lax.dynamic_slice_in_dim(l_scaled, col_pos * count, count, 1)
    lfull = gather(share, nrow, nchip, 1).reshape(NSUP, total, W)

    rows = tile_lists - row_pos * tile_rows
    rows = jnp.where((rows >= 0) & (rows < tile_rows), rows, -1)
    cols = tile_lists - col_pos * tile_cols
    cols = jnp.where((cols >= 0) & (cols < tile_cols), cols, -1)
    rows = jnp.where(jnp.max(cols, axis=1, keepdims=True) >= 0, rows, -1)
    partial, terms = products(rows, cols, ancestor_inv, lfull)

    sums = [
        partial.reshape(NSUP, nrow, nchip, 2, count, W),
        terms.reshape(NSUP, nrow, nchip, 2, part, W),
    ]
    sums = scatter(sums, "core", 2, 3, 2)
    sums = scatter(sums, "chip", nchip, 2, 3)
    mine, term = scatter(sums, "row", nrow, 1, 4)
    diag = gather(term, nrow, nchip, 5).reshape(NSUP, W, W)
    return mine, diag_inv - diag


def solution(mesh):
    placed = (P("prow", "pcol"), P(None, "prow", None), P(), P())
    return jax.shard_map(
        functools.partial(per_device, mesh.shape["prow"], mesh.shape["pcol"]),
        mesh=mesh,
        in_specs=placed,
        out_specs=(P(None, ("prow", "pcol"), None), P()),
        check_vma=False,
    )
```

```python
import functools

import jax
import jax.numpy as jnp
from jax import lax
from jax.experimental import pallas as pl
from jax.experimental.pallas import tpu as pltpu
from jax.sharding import PartitionSpec as P

TILE = 256
W = 512
NS = 6
NSUP = 2
MESH = pl.DeviceIdType.MESH


def place(stage):
    row = lax.axis_index("prow")
    col = lax.axis_index("pcol")
    core = lax.rem(col, 2)
    chip = col // 2
    if stage == "row":
        return row, lambda m: (m, col)
    if stage == "chip":
        return chip, lambda m: (row, m * 2 + core)
    return core, lambda m: (row, chip * 2 + m)


def enter(peers):
    barrier = pltpu.get_barrier_semaphore()
    for peer in peers:
        pl.semaphore_signal(barrier, inc=1, device_id=peer, device_id_type=MESH)
    pl.semaphore_wait(barrier, len(peers))


def others(stage, size):
    me, device = place(stage)
    return [device(lax.rem(me + step, size)) for step in range(1, size)]


def send(src, dst, send_sem, recv_sem, peer):
    copy = pltpu.make_async_remote_copy(
        src_ref=src,
        dst_ref=dst,
        send_sem=send_sem,
        recv_sem=recv_sem,
        device_id=peer,
        device_id_type=MESH,
    )
    copy.start()
    return copy


def scatter_kernel(
    nrow, nchip, x_ref, y_ref, x_out, y_out, core_x, core_y, held, chip_in, sums, row_in, *sems
):
    core_send, core_recv, chip_send, chip_recv, row_send, row_recv = sems
    row, _ = place("row")
    chip, _ = place("chip")
    core, _ = place("core")
    rows, chips, cores = others("row", nrow), others("chip", nchip), others("core", 2)
    enter(rows + chips + cores)
    count = x_ref.shape[-2]
    pieces = [(step, sup) for step in [*range(1, nrow), 0] for sup in range(NSUP)]
    owners = [lax.rem(row + step, nrow) for step, _ in pieces]
    from_core = []
    for at, (_, sup) in enumerate(pieces):
        to = owners[at]
        from_core.append(
            [
                send(
                    src.at[sup, to, :, 1 - core],
                    dst.at[at],
                    core_send.at[at, which],
                    core_recv.at[at, which],
                    cores[0],
                )
                for which, (src, dst) in enumerate(((x_ref, core_x), (y_ref, core_y)))
            ]
        )
    from_chips = []
    from_rows = []

    def finish(at):
        step, sup = pieces[at]
        for copy in from_chips[at]:
            copy.wait_recv()
        total = held[at, chip]
        for near in range(nchip - 1):
            total += chip_in[at, near]
        sums[at] = total
        if step > 0:
            from_rows.append(
                send(
                    sums.at[at],
                    row_in.at[at],
                    row_send.at[at],
                    row_recv.at[at],
                    rows[step - 1],
                )
            )

    for at, (_, sup) in enumerate(pieces):
        for copy in from_core[at]:
            copy.wait_recv()
        held[at, :, :count] = x_ref[sup, owners[at], :, core] + core_x[at]
        held[at, :, count:] = y_ref[sup, owners[at], :, core] + core_y[at]
        from_chips.append(
            [
                send(
                    held.at[at, lax.rem(chip + near + 1, nchip)],
                    chip_in.at[at, near],
                    chip_send.at[at, near],
                    chip_recv.at[at, near],
                    peer,
                )
                for near, peer in enumerate(chips)
            ]
        )
        if at >= 2:
            finish(at - 2)
    finish(len(pieces) - 2)
    finish(len(pieces) - 1)
    for copy in from_rows:
        copy.wait_recv()
    for sup in range(NSUP):
        total = sums[(nrow - 1) * NSUP + sup]
        for step in range(nrow - 1):
            total += row_in[step * NSUP + sup]
        x_out[sup] = total[:count]
        y_out[sup] = total[count:]
    for group in from_core + from_chips + [from_rows]:
        for copy in group:
            copy.wait_send()


def scatter(x, y, nrow, nchip, collective_id):
    count, part = x.shape[-2], y.shape[-2]
    n = nrow * NSUP
    f32 = jnp.float32
    vmem = pl.BlockSpec(memory_space=pltpu.VMEM)
    core, chip, row = (n, 2), (n, nchip - 1), (n - NSUP,)
    return pl.pallas_call(
        functools.partial(scatter_kernel, nrow, nchip),
        out_shape=[
            jax.ShapeDtypeStruct((NSUP, count, W), f32),
            jax.ShapeDtypeStruct((NSUP, part, W), f32),
        ],
        in_specs=[vmem, vmem],
        out_specs=[vmem, vmem],
        scratch_shapes=[
            pltpu.VMEM((n, nchip, count, W), f32),
            pltpu.VMEM((n, nchip, part, W), f32),
            pltpu.VMEM((n, nchip, count + part, W), f32),
            pltpu.VMEM((n, nchip - 1, count + part, W), f32),
            pltpu.VMEM((n, count + part, W), f32),
            pltpu.VMEM((n - NSUP, count + part, W), f32),
            *(pltpu.SemaphoreType.DMA(s) for s in (core, core, chip, chip, row, row)),
        ],
        compiler_params=pltpu.CompilerParams(
            collective_id=collective_id,
            has_side_effects=True,
            vmem_limit_bytes=44 * 1024 * 1024,
        ),
    )(x, y)


def gather_kernel(nrow, nchip, x_ref, out_ref, *sems):
    row_send, row_recv, chip_send, chip_recv, core_send, core_recv = sems
    row, _ = place("row")
    chip, _ = place("chip")
    core, _ = place("core")
    rows, chips, cores = others("row", nrow), others("chip", nchip), others("core", 2)
    enter(rows + chips + cores)
    started = []

    def forward(*args):
        started.append(send(*args))
        return started[-1]

    mine = out_ref.at[:, row, chip, core]
    from_rows = [
        forward(x_ref, mine, row_send.at[step], row_recv.at[step], peer)
        for step, peer in enumerate(rows)
    ]
    from_chips = []
    last = []
    for near in range(nrow):
        src = x_ref
        slot = mine
        if near > 0:
            from_rows[near - 1].wait_recv()
            slot = out_ref.at[:, lax.rem(row - near + nrow, nrow), chip, core]
            src = slot
        for step, peer in enumerate(chips):
            from_chips.append(
                (
                    near,
                    step + 1,
                    forward(src, slot, chip_send.at[step, near], chip_recv.at[step, near], peer),
                )
            )
        last.append(forward(src, slot, core_send.at[0, near], core_recv.at[0, near], cores[0]))
    for near, step, copy in from_chips:
        copy.wait_recv()
        slot = out_ref.at[
            :, lax.rem(row - near + nrow, nrow), lax.rem(chip - step + nchip, nchip), core
        ]
        last.append(
            forward(slot, slot, core_send.at[step, near], core_recv.at[step, near], cores[0])
        )
    for copy in last:
        copy.wait_recv()
    for copy in started:
        copy.wait_send()


def gather(x, nrow, nchip, collective_id):
    shape = (x.shape[0], nrow, nchip, 2) + x.shape[1:]
    row, chip, core = ((nrow - 1,), (nchip - 1, nrow), (nchip, nrow))
    full = pl.pallas_call(
        functools.partial(gather_kernel, nrow, nchip),
        out_shape=jax.ShapeDtypeStruct(shape, x.dtype),
        in_specs=[pl.BlockSpec(memory_space=pl.ANY)],
        out_specs=pl.BlockSpec(memory_space=pl.ANY),
        scratch_shapes=[
            pltpu.SemaphoreType.DMA(n) for n in (row, row, chip, chip, core, core)
        ],
        compiler_params=pltpu.CompilerParams(
            collective_id=collective_id, has_side_effects=True
        ),
    )(x)
    where = (0, place("row")[0], place("chip")[0], place("core")[0], 0, 0)
    return lax.dynamic_update_slice(full, x[:, None, None, None], where)


def product_kernel(rows_ref, cols_ref, a_ref, l_ref, p_ref, d_ref):
    sup, i, j = pl.program_id(0), pl.program_id(1), pl.program_id(2)
    highest = lax.Precision.HIGHEST
    row_hit = rows_ref[sup, i] >= 0

    @pl.when((i == 0) & (j == 0))
    def _():
        d_ref[...] = jnp.zeros_like(d_ref)

    @pl.when(j == 0)
    def _():
        p_ref[...] = jnp.zeros_like(p_ref)

    @pl.when(row_hit & (cols_ref[sup, j] >= 0))
    def _():
        block = l_ref[0, pl.ds(pl.multiple_of(j * TILE, TILE), TILE), :]
        p_ref[0] -= jnp.dot(
            a_ref[...], block, precision=highest, preferred_element_type=jnp.float32
        )

    @pl.when(row_hit & (j == NS - 1))
    def _():
        block = l_ref[0, pl.ds(pl.multiple_of(i * TILE, TILE), TILE), :]
        d_ref[0] += lax.dot_general(
            block,
            p_ref[0],
            (((0,), (0,)), ((), ())),
            precision=highest,
            preferred_element_type=jnp.float32,
        )


def products(rows, cols, ancestor, lfull):
    def a_map(sup, i, j, rows_ref, cols_ref):
        row, col = rows_ref[sup, i], cols_ref[sup, j]
        hit = (row >= 0) & (col >= 0)
        return jnp.where(hit, row, 0), jnp.where(hit, col, 0)

    total = lfull.shape[1]
    return pl.pallas_call(
        product_kernel,
        out_shape=(
            jax.ShapeDtypeStruct((NSUP, total, W), jnp.float32),
            jax.ShapeDtypeStruct((NSUP, W, W), jnp.float32),
        ),
        grid_spec=pltpu.PrefetchScalarGridSpec(
            num_scalar_prefetch=2,
            grid=(NSUP, NS, NS),
            in_specs=[
                pl.BlockSpec((TILE, TILE), a_map),
                pl.BlockSpec((1, total, W), lambda sup, i, j, *_: (sup, 0, 0)),
            ],
            out_specs=[
                pl.BlockSpec((1, TILE, W), lambda sup, i, j, *_: (sup, i, 0)),
                pl.BlockSpec((1, W, W), lambda sup, i, j, *_: (sup, 0, 0)),
            ],
        ),
        compiler_params=pltpu.CompilerParams(vmem_limit_bytes=40 * 1024 * 1024),
    )(rows, cols, ancestor, lfull)


def per_device(nrow, ncol, ancestor_inv, l_scaled, diag_inv, tile_lists):
    nchip = ncol // 2
    tile_rows = ancestor_inv.shape[0] // TILE
    tile_cols = ancestor_inv.shape[1] // TILE
    row_pos = lax.axis_index("prow")
    col_pos = lax.axis_index("pcol")
    count = l_scaled.shape[1] // ncol
    part = W // (nrow * ncol)
    total = l_scaled.shape[1] * nrow

    share = lax.dynamic_slice_in_dim(l_scaled, col_pos * count, count, 1)
    lfull = gather(share, nrow, nchip, 1).reshape(NSUP, total, W)

    rows = tile_lists - row_pos * tile_rows
    rows = jnp.where((rows >= 0) & (rows < tile_rows), rows, -1)
    cols = tile_lists - col_pos * tile_cols
    cols = jnp.where((cols >= 0) & (cols < tile_cols), cols, -1)
    rows = jnp.where(jnp.max(cols, axis=1, keepdims=True) >= 0, rows, -1)
    partial, terms = products(rows, cols, ancestor_inv, lfull)

    mine, term = scatter(
        partial.reshape(NSUP, nrow, nchip, 2, count, W),
        terms.reshape(NSUP, nrow, nchip, 2, part, W),
        nrow,
        nchip,
        2,
    )
    diag = gather(term, nrow, nchip, 5).reshape(NSUP, W, W)
    return mine, diag_inv - diag


def solution(mesh):
    placed = (P("prow", "pcol"), P(None, "prow", None), P(), P())
    return jax.shard_map(
        functools.partial(per_device, mesh.shape["prow"], mesh.shape["pcol"]),
        mesh=mesh,
        in_specs=placed,
        out_specs=(P(None, ("prow", "pcol"), None), P()),
        check_vma=False,
    )
```

```python
import functools

import jax
import jax.numpy as jnp
from jax import lax
from jax.experimental import pallas as pl
from jax.experimental.pallas import tpu as pltpu
from jax.sharding import PartitionSpec as P

TILE = 256
W = 512
NS = 6
NSUP = 2
MESH = pl.DeviceIdType.MESH


def place(stage):
    row = lax.axis_index("prow")
    col = lax.axis_index("pcol")
    core = lax.rem(col, 2)
    chip = col // 2
    if stage == "row":
        return row, lambda m: (m, col)
    if stage == "chip":
        return chip, lambda m: (row, m * 2 + core)
    return core, lambda m: (row, chip * 2 + m)


def enter(peers):
    barrier = pltpu.get_barrier_semaphore()
    for peer in peers:
        pl.semaphore_signal(barrier, inc=1, device_id=peer, device_id_type=MESH)
    pl.semaphore_wait(barrier, len(peers))


def others(stage, size):
    me, device = place(stage)
    return [device(lax.rem(me + step, size)) for step in range(1, size)]


def send(src, dst, send_sem, recv_sem, peer):
    copy = pltpu.make_async_remote_copy(
        src_ref=src,
        dst_ref=dst,
        send_sem=send_sem,
        recv_sem=recv_sem,
        device_id=peer,
        device_id_type=MESH,
    )
    copy.start()
    return copy


def scatter_kernel(
    nrow, nchip, x_ref, y_ref, x_out, y_out, core_x, core_y, held, chip_in, sums, row_in, *sems
):
    core_send, core_recv, chip_send, chip_recv, row_send, row_recv = sems
    row, _ = place("row")
    chip, _ = place("chip")
    core, _ = place("core")
    rows, chips, cores = others("row", nrow), others("chip", nchip), others("core", 2)
    enter(rows + chips + cores)
    count = x_ref.shape[-2]
    pieces = [(step, sup) for step in [*range(1, nrow), 0] for sup in range(NSUP)]
    owners = [lax.rem(row + step, nrow) for step, _ in pieces]
    from_core = []
    for at, (_, sup) in enumerate(pieces):
        to = owners[at]
        from_core.append(
            [
                send(
                    src.at[sup, to, :, 1 - core],
                    dst.at[at],
                    core_send.at[at, which],
                    core_recv.at[at, which],
                    cores[0],
                )
                for which, (src, dst) in enumerate(((x_ref, core_x), (y_ref, core_y)))
            ]
        )
    from_chips = []
    from_rows = []

    def finish(at):
        step, sup = pieces[at]
        for copy in from_chips[at]:
            copy.wait_recv()
        total = held[at, chip]
        for near in range(nchip - 1):
            total += chip_in[at, near]
        sums[at] = total
        if step > 0:
            from_rows.append(
                send(
                    sums.at[at],
                    row_in.at[at],
                    row_send.at[at],
                    row_recv.at[at],
                    rows[step - 1],
                )
            )

    for at, (_, sup) in enumerate(pieces):
        for copy in from_core[at]:
            copy.wait_recv()
        held[at, :, :count] = x_ref[sup, owners[at], :, core] + core_x[at]
        held[at, :, count:] = y_ref[sup, owners[at], :, core] + core_y[at]
        from_chips.append(
            [
                send(
                    held.at[at, lax.rem(chip + near + 1, nchip)],
                    chip_in.at[at, near],
                    chip_send.at[at, near],
                    chip_recv.at[at, near],
                    peer,
                )
                for near, peer in enumerate(chips)
            ]
        )
        if at >= 2:
            finish(at - 2)
    finish(len(pieces) - 2)
    finish(len(pieces) - 1)
    for copy in from_rows:
        copy.wait_recv()
    for sup in range(NSUP):
        total = sums[(nrow - 1) * NSUP + sup]
        for step in range(nrow - 1):
            total += row_in[step * NSUP + sup]
        x_out[sup] = total[:count]
        y_out[sup] = total[count:]
    for group in from_core + from_chips + [from_rows]:
        for copy in group:
            copy.wait_send()


def scatter(x, y, nrow, nchip, collective_id):
    count, part = x.shape[-2], y.shape[-2]
    n = nrow * NSUP
    f32 = jnp.float32
    vmem = pl.BlockSpec(memory_space=pltpu.VMEM)
    core, chip, row = (n, 2), (n, nchip - 1), (n - NSUP,)
    return pl.pallas_call(
        functools.partial(scatter_kernel, nrow, nchip),
        out_shape=[
            jax.ShapeDtypeStruct((NSUP, count, W), f32),
            jax.ShapeDtypeStruct((NSUP, part, W), f32),
        ],
        in_specs=[vmem, vmem],
        out_specs=[vmem, vmem],
        scratch_shapes=[
            pltpu.VMEM((n, nchip, count, W), f32),
            pltpu.VMEM((n, nchip, part, W), f32),
            pltpu.VMEM((n, nchip, count + part, W), f32),
            pltpu.VMEM((n, nchip - 1, count + part, W), f32),
            pltpu.VMEM((n, count + part, W), f32),
            pltpu.VMEM((n - NSUP, count + part, W), f32),
            *(pltpu.SemaphoreType.DMA(s) for s in (core, core, chip, chip, row, row)),
        ],
        compiler_params=pltpu.CompilerParams(
            collective_id=collective_id,
            has_side_effects=True,
            vmem_limit_bytes=44 * 1024 * 1024,
        ),
    )(x, y)


def gather_kernel(nrow, nchip, x_ref, out_ref, *sems):
    row_send, row_recv, chip_send, chip_recv, core_send, core_recv = sems
    row, _ = place("row")
    chip, _ = place("chip")
    core, _ = place("core")
    rows, chips, cores = others("row", nrow), others("chip", nchip), others("core", 2)
    enter(rows + chips + cores)
    started = []

    def forward(*args):
        started.append(send(*args))
        return started[-1]

    mine = out_ref.at[:, row, chip, core]
    from_rows = [
        forward(x_ref, mine, row_send.at[step], row_recv.at[step], peer)
        for step, peer in enumerate(rows)
    ]
    from_chips = []
    last = []
    for near in range(nrow):
        src = x_ref
        slot = mine
        if near > 0:
            from_rows[near - 1].wait_recv()
            slot = out_ref.at[:, lax.rem(row - near + nrow, nrow), chip, core]
            src = slot
        for step, peer in enumerate(chips):
            from_chips.append(
                (
                    near,
                    step + 1,
                    forward(src, slot, chip_send.at[step, near], chip_recv.at[step, near], peer),
                )
            )
        last.append(forward(src, slot, core_send.at[0, near], core_recv.at[0, near], cores[0]))
    for near, step, copy in from_chips:
        copy.wait_recv()
        slot = out_ref.at[
            :, lax.rem(row - near + nrow, nrow), lax.rem(chip - step + nchip, nchip), core
        ]
        last.append(
            forward(slot, slot, core_send.at[step, near], core_recv.at[step, near], cores[0])
        )
    for copy in last:
        copy.wait_recv()
    for copy in started:
        copy.wait_send()


def gather(x, nrow, nchip, collective_id):
    shape = (x.shape[0], nrow, nchip, 2) + x.shape[1:]
    row, chip, core = ((nrow - 1,), (nchip - 1, nrow), (nchip, nrow))
    full = pl.pallas_call(
        functools.partial(gather_kernel, nrow, nchip),
        out_shape=jax.ShapeDtypeStruct(shape, x.dtype),
        in_specs=[pl.BlockSpec(memory_space=pl.ANY)],
        out_specs=pl.BlockSpec(memory_space=pl.ANY),
        scratch_shapes=[
            pltpu.SemaphoreType.DMA(n) for n in (row, row, chip, chip, core, core)
        ],
        compiler_params=pltpu.CompilerParams(
            collective_id=collective_id, has_side_effects=True
        ),
    )(x)
    where = (0, place("row")[0], place("chip")[0], place("core")[0], 0, 0)
    return lax.dynamic_update_slice(full, x[:, None, None, None], where)


def dot(a, b, contract):
    def split(x):
        high = x.astype(jnp.bfloat16)
        return high, (x - high.astype(jnp.float32)).astype(jnp.bfloat16)

    def one(x, y):
        return lax.dot_general(
            x, y, ((contract, (0,)), ((), ())), preferred_element_type=jnp.float32
        )

    a_high, a_low = split(a)
    b_high, b_low = split(b)
    return one(a_low, b_high) + one(a_high, b_low) + one(a_high, b_high)


def product_kernel(rows_ref, cols_ref, *refs):
    *tiles, l_ref, p_ref, d_ref = refs
    sup, i = pl.program_id(0), pl.program_id(1)
    row_hit = rows_ref[sup, i] >= 0

    @pl.when(i == 0)
    def _():
        d_ref[...] = jnp.zeros_like(d_ref)

    p_ref[...] = jnp.zeros_like(p_ref)

    @pl.when(row_hit)
    def _():
        for j, a_ref in enumerate(tiles):

            @pl.when(cols_ref[sup, j] >= 0)
            def _():
                p_ref[0] -= dot(a_ref[...], l_ref[0, j * TILE:(j + 1) * TILE, :], (1,))

        block = l_ref[0, pl.ds(pl.multiple_of(i * TILE, TILE), TILE), :]
        d_ref[0] += dot(block, p_ref[0], (0,))


def products(rows, cols, ancestor, lfull):
    def tile(j):
        def index(sup, i, rows_ref, cols_ref):
            row, col = rows_ref[sup, i], cols_ref[sup, j]
            hit = (row >= 0) & (col >= 0)
            return jnp.where(hit, row, 0), jnp.where(hit, col, 0)

        return pl.BlockSpec((TILE, TILE), index)

    total = lfull.shape[1]
    return pl.pallas_call(
        product_kernel,
        out_shape=(
            jax.ShapeDtypeStruct((NSUP, total, W), jnp.float32),
            jax.ShapeDtypeStruct((NSUP, W, W), jnp.float32),
        ),
        grid_spec=pltpu.PrefetchScalarGridSpec(
            num_scalar_prefetch=2,
            grid=(NSUP, NS),
            in_specs=[tile(j) for j in range(NS)]
            + [pl.BlockSpec((1, total, W), lambda sup, i, *_: (sup, 0, 0))],
            out_specs=[
                pl.BlockSpec((1, TILE, W), lambda sup, i, *_: (sup, i, 0)),
                pl.BlockSpec((1, W, W), lambda sup, i, *_: (sup, 0, 0)),
            ],
        ),
        compiler_params=pltpu.CompilerParams(vmem_limit_bytes=40 * 1024 * 1024),
    )(rows, cols, *[ancestor] * NS, lfull)


def per_device(nrow, ncol, ancestor_inv, l_scaled, diag_inv, tile_lists):
    nchip = ncol // 2
    tile_rows = ancestor_inv.shape[0] // TILE
    tile_cols = ancestor_inv.shape[1] // TILE
    row_pos = lax.axis_index("prow")
    col_pos = lax.axis_index("pcol")
    count = l_scaled.shape[1] // ncol
    part = W // (nrow * ncol)
    total = l_scaled.shape[1] * nrow

    share = lax.dynamic_slice_in_dim(l_scaled, col_pos * count, count, 1)
    lfull = gather(share, nrow, nchip, 1).reshape(NSUP, total, W)

    rows = tile_lists - row_pos * tile_rows
    rows = jnp.where((rows >= 0) & (rows < tile_rows), rows, -1)
    cols = tile_lists - col_pos * tile_cols
    cols = jnp.where((cols >= 0) & (cols < tile_cols), cols, -1)
    rows = jnp.where(jnp.max(cols, axis=1, keepdims=True) >= 0, rows, -1)
    partial, terms = products(rows, cols, ancestor_inv, lfull)

    mine, term = scatter(
        partial.reshape(NSUP, nrow, nchip, 2, count, W),
        terms.reshape(NSUP, nrow, nchip, 2, part, W),
        nrow,
        nchip,
        2,
    )
    diag = gather(term, nrow, nchip, 5).reshape(NSUP, W, W)
    return mine, diag_inv - diag


def solution(mesh):
    placed = (P("prow", "pcol"), P(None, "prow", None), P(), P())
    return jax.shard_map(
        functools.partial(per_device, mesh.shape["prow"], mesh.shape["pcol"]),
        mesh=mesh,
        in_specs=placed,
        out_specs=(P(None, ("prow", "pcol"), None), P()),
        check_vma=False,
    )
```

```python
import functools

import jax
import jax.numpy as jnp
from jax import lax
from jax.experimental import pallas as pl
from jax.experimental.pallas import tpu as pltpu
from jax.sharding import PartitionSpec as P

TILE = 256
W = 512
NS = 6
NSUP = 2
MESH = pl.DeviceIdType.MESH


def place(stage):
    row = lax.axis_index("prow")
    col = lax.axis_index("pcol")
    core = lax.rem(col, 2)
    chip = col // 2
    if stage == "row":
        return row, lambda m: (m, col)
    if stage == "chip":
        return chip, lambda m: (row, m * 2 + core)
    return core, lambda m: (row, chip * 2 + m)


def enter(peers):
    barrier = pltpu.get_barrier_semaphore()
    for peer in peers:
        pl.semaphore_signal(barrier, inc=1, device_id=peer, device_id_type=MESH)
    pl.semaphore_wait(barrier, len(peers))


def others(stage, size):
    me, device = place(stage)
    return [device(lax.rem(me + step, size)) for step in range(1, size)]


def send(src, dst, send_sem, recv_sem, peer):
    copy = pltpu.make_async_remote_copy(
        src_ref=src,
        dst_ref=dst,
        send_sem=send_sem,
        recv_sem=recv_sem,
        device_id=peer,
        device_id_type=MESH,
    )
    copy.start()
    return copy


def scatter_kernel(
    nrow, nchip, x_ref, y_ref, x_out, y_out, core_x, core_y, held, chip_in, sums, row_in, *sems
):
    core_send, core_recv, chip_send, chip_recv, row_send, row_recv = sems
    row, _ = place("row")
    chip, _ = place("chip")
    core, _ = place("core")
    rows, chips, cores = others("row", nrow), others("chip", nchip), others("core", 2)
    enter(rows + chips + cores)
    count = x_ref.shape[-2]
    pieces = [(step, sup) for step in [*range(1, nrow), 0] for sup in range(NSUP)]
    owners = [lax.rem(row + step, nrow) for step, _ in pieces]
    from_core = []
    for at, (_, sup) in enumerate(pieces):
        to = owners[at]
        from_core.append(
            [
                send(
                    src.at[sup, to, :, 1 - core],
                    dst.at[at],
                    core_send.at[at, which],
                    core_recv.at[at, which],
                    cores[0],
                )
                for which, (src, dst) in enumerate(((x_ref, core_x), (y_ref, core_y)))
            ]
        )
    from_chips = []
    from_rows = []

    def finish(at):
        step, sup = pieces[at]
        for copy in from_chips[at]:
            copy.wait_recv()
        total = held[at, chip]
        for near in range(nchip - 1):
            total += chip_in[at, near]
        sums[at] = total
        if step > 0:
            from_rows.append(
                send(
                    sums.at[at],
                    row_in.at[at],
                    row_send.at[at],
                    row_recv.at[at],
                    rows[step - 1],
                )
            )

    for at, (_, sup) in enumerate(pieces):
        for copy in from_core[at]:
            copy.wait_recv()
        held[at, :, :count] = x_ref[sup, owners[at], :, core] + core_x[at]
        held[at, :, count:] = y_ref[sup, owners[at], :, core] + core_y[at]
        from_chips.append(
            [
                send(
                    held.at[at, lax.rem(chip + near + 1, nchip)],
                    chip_in.at[at, near],
                    chip_send.at[at, near],
                    chip_recv.at[at, near],
                    peer,
                )
                for near, peer in enumerate(chips)
            ]
        )
        if at >= 2:
            finish(at - 2)
    finish(len(pieces) - 2)
    finish(len(pieces) - 1)
    for copy in from_rows:
        copy.wait_recv()
    for sup in range(NSUP):
        total = sums[(nrow - 1) * NSUP + sup]
        for step in range(nrow - 1):
            total += row_in[step * NSUP + sup]
        x_out[sup] = total[:count]
        y_out[sup] = total[count:]
    for group in from_core + from_chips + [from_rows]:
        for copy in group:
            copy.wait_send()


def scatter(x, y, nrow, nchip, collective_id):
    count, part = x.shape[-2], y.shape[-2]
    n = nrow * NSUP
    f32 = jnp.float32
    vmem = pl.BlockSpec(memory_space=pltpu.VMEM)
    core, chip, row = (n, 2), (n, nchip - 1), (n - NSUP,)
    return pl.pallas_call(
        functools.partial(scatter_kernel, nrow, nchip),
        out_shape=[
            jax.ShapeDtypeStruct((NSUP, count, W), f32),
            jax.ShapeDtypeStruct((NSUP, part, W), f32),
        ],
        in_specs=[vmem, vmem],
        out_specs=[vmem, vmem],
        scratch_shapes=[
            pltpu.VMEM((n, nchip, count, W), f32),
            pltpu.VMEM((n, nchip, part, W), f32),
            pltpu.VMEM((n, nchip, count + part, W), f32),
            pltpu.VMEM((n, nchip - 1, count + part, W), f32),
            pltpu.VMEM((n, count + part, W), f32),
            pltpu.VMEM((n - NSUP, count + part, W), f32),
            *(pltpu.SemaphoreType.DMA(s) for s in (core, core, chip, chip, row, row)),
        ],
        compiler_params=pltpu.CompilerParams(
            collective_id=collective_id,
            has_side_effects=True,
            vmem_limit_bytes=44 * 1024 * 1024,
        ),
    )(x, y)


def gather_kernel(nrow, nchip, known, x_ref, out_ref, *sems):
    row_send, row_recv, chip_send, chip_recv, core_send, core_recv = sems
    row, _ = place("row")
    chip, _ = place("chip")
    core, _ = place("core")
    rows, chips, cores = others("row", nrow), others("chip", nchip), others("core", 2)
    enter(rows + chips + cores)
    started = []

    def forward(*args):
        started.append(send(*args))
        return started[-1]

    mine = out_ref.at[:, row, chip, core]
    from_rows = [
        forward(x_ref, mine, row_send.at[step], row_recv.at[step], peer)
        for step, peer in enumerate(rows)
    ]
    from_chips = []
    last = []
    for near in range(1 if known else 0, nrow):
        src = x_ref
        slot = mine
        if near > 0:
            from_rows[near - 1].wait_recv()
            slot = out_ref.at[:, lax.rem(row - near + nrow, nrow), chip, core]
            src = slot
        for step, peer in enumerate(chips):
            from_chips.append(
                (
                    near,
                    step + 1,
                    forward(src, slot, chip_send.at[step, near], chip_recv.at[step, near], peer),
                )
            )
        last.append(forward(src, slot, core_send.at[0, near], core_recv.at[0, near], cores[0]))
    for near, step, copy in from_chips:
        copy.wait_recv()
        slot = out_ref.at[
            :, lax.rem(row - near + nrow, nrow), lax.rem(chip - step + nchip, nchip), core
        ]
        last.append(
            forward(slot, slot, core_send.at[step, near], core_recv.at[step, near], cores[0])
        )
    for copy in last:
        copy.wait_recv()
    for copy in started:
        copy.wait_send()


def gather(x, nrow, nchip, collective_id, plane=None):
    shape = (x.shape[0], nrow, nchip, 2) + x.shape[1:]
    row, chip, core = ((nrow - 1,), (nchip - 1, nrow), (nchip, nrow))
    full = pl.pallas_call(
        functools.partial(gather_kernel, nrow, nchip, plane is not None),
        out_shape=jax.ShapeDtypeStruct(shape, x.dtype),
        in_specs=[pl.BlockSpec(memory_space=pl.ANY)],
        out_specs=pl.BlockSpec(memory_space=pl.ANY),
        scratch_shapes=[
            pltpu.SemaphoreType.DMA(n) for n in (row, row, chip, chip, core, core)
        ],
        compiler_params=pltpu.CompilerParams(
            collective_id=collective_id, has_side_effects=True
        ),
    )(x)
    if plane is not None:
        plane = plane.reshape(x.shape[0], 1, nchip, 2, *x.shape[1:])
        return lax.dynamic_update_slice(full, plane, (0, place("row")[0], 0, 0, 0, 0))
    where = (0, place("row")[0], place("chip")[0], place("core")[0], 0, 0)
    return lax.dynamic_update_slice(full, x[:, None, None, None], where)


def dot(a, b, contract):
    def split(x):
        high = x.astype(jnp.bfloat16)
        return high, (x - high.astype(jnp.float32)).astype(jnp.bfloat16)

    def one(x, y):
        return lax.dot_general(
            x, y, ((contract, (0,)), ((), ())), preferred_element_type=jnp.float32
        )

    a_high, a_low = split(a)
    b_high, b_low = split(b)
    return one(a_low, b_high) + one(a_high, b_low) + one(a_high, b_high)


def product_kernel(rows_ref, cols_ref, *refs):
    *tiles, l_ref, p_ref, d_ref = refs
    sup, i = pl.program_id(0), pl.program_id(1)
    row_hit = rows_ref[sup, i] >= 0

    @pl.when(i == 0)
    def _():
        d_ref[...] = jnp.zeros_like(d_ref)

    p_ref[...] = jnp.zeros_like(p_ref)

    @pl.when(row_hit)
    def _():
        for j, a_ref in enumerate(tiles):

            @pl.when(cols_ref[sup, j] >= 0)
            def _():
                p_ref[0] -= dot(a_ref[...], l_ref[0, j * TILE:(j + 1) * TILE, :], (1,))

        block = l_ref[0, pl.ds(pl.multiple_of(i * TILE, TILE), TILE), :]
        d_ref[0] += dot(block, p_ref[0], (0,))


def products(rows, cols, ancestor, lfull):
    def tile(j):
        def index(sup, i, rows_ref, cols_ref):
            row, col = rows_ref[sup, i], cols_ref[sup, j]
            hit = (row >= 0) & (col >= 0)
            return jnp.where(hit, row, 0), jnp.where(hit, col, 0)

        return pl.BlockSpec((TILE, TILE), index)

    total = lfull.shape[1]
    return pl.pallas_call(
        product_kernel,
        out_shape=(
            jax.ShapeDtypeStruct((NSUP, total, W), jnp.float32),
            jax.ShapeDtypeStruct((NSUP, W, W), jnp.float32),
        ),
        grid_spec=pltpu.PrefetchScalarGridSpec(
            num_scalar_prefetch=2,
            grid=(NSUP, NS),
            in_specs=[tile(j) for j in range(NS)]
            + [pl.BlockSpec((1, total, W), lambda sup, i, *_: (sup, 0, 0))],
            out_specs=[
                pl.BlockSpec((1, TILE, W), lambda sup, i, *_: (sup, i, 0)),
                pl.BlockSpec((1, W, W), lambda sup, i, *_: (sup, 0, 0)),
            ],
        ),
        compiler_params=pltpu.CompilerParams(vmem_limit_bytes=40 * 1024 * 1024),
    )(rows, cols, *[ancestor] * NS, lfull)


def per_device(nrow, ncol, ancestor_inv, l_scaled, diag_inv, tile_lists):
    nchip = ncol // 2
    tile_rows = ancestor_inv.shape[0] // TILE
    tile_cols = ancestor_inv.shape[1] // TILE
    row_pos = lax.axis_index("prow")
    col_pos = lax.axis_index("pcol")
    count = l_scaled.shape[1] // ncol
    part = W // (nrow * ncol)
    total = l_scaled.shape[1] * nrow

    share = lax.dynamic_slice_in_dim(l_scaled, col_pos * count, count, 1)
    lfull = gather(share, nrow, nchip, 1, l_scaled).reshape(NSUP, total, W)

    rows = tile_lists - row_pos * tile_rows
    rows = jnp.where((rows >= 0) & (rows < tile_rows), rows, -1)
    cols = tile_lists - col_pos * tile_cols
    cols = jnp.where((cols >= 0) & (cols < tile_cols), cols, -1)
    rows = jnp.where(jnp.max(cols, axis=1, keepdims=True) >= 0, rows, -1)
    partial, terms = products(rows, cols, ancestor_inv, lfull)

    mine, term = scatter(
        partial.reshape(NSUP, nrow, nchip, 2, count, W),
        terms.reshape(NSUP, nrow, nchip, 2, part, W),
        nrow,
        nchip,
        2,
    )
    diag = gather(term, nrow, nchip, 5).reshape(NSUP, W, W)
    return mine, diag_inv - diag


def solution(mesh):
    placed = (P("prow", "pcol"), P(None, "prow", None), P(), P())
    return jax.shard_map(
        functools.partial(per_device, mesh.shape["prow"], mesh.shape["pcol"]),
        mesh=mesh,
        in_specs=placed,
        out_specs=(P(None, ("prow", "pcol"), None), P()),
        check_vma=False,
    )
```
